32 devices in a mesh: sub: 16 (over z, y, x), rng: 2 (over core).
Axes of the slice: x: 2, y: 2, z: 4, core: 2. Of those that a mesh axis runs over, the one named last changes fastest.
Arguments:
- raw_echoes: bfloat16 [2048, 2, 16384], P('sub', None, 'rng'), may hold values from -6 to 6
- chirp_replica: bfloat16 [2, 512], replicated, may hold values from -0.1875 to 0.1875
- steering: bfloat16 [16, 2, 128, 128], P('sub'), may hold values from -0.375 to 0.375
- band_start: int32 [4, 16, 2, 128], P(None, 'sub'), may hold values from 0 to 120
- band_coef: bfloat16 [4, 16, 2, 2, 8, 128], P(None, 'sub'), may hold values from -1 to 1
- phase_rate: float32 [4, 16, 128], P(None, 'sub'), may hold values from -8 to 8
- range_map: bfloat16 [2, 8192, 256], P(None, 'rng'), may hold values from -0.0625 to 0.0625
- slot_maps: bfloat16 [512, 2, 32, 128], P(('sub', 'rng')), may hold values from -0.09375 to 0.09375
- coverage: int32 [512, 1], P(('sub', 'rng')), may hold values from 0 to 31, as said below
Outputs:
- ground_tiles: float32 [32, 2, 32, 256], P(('sub', 'rng'))
The draws below stay inside these ranges and needn't reach their ends.
Inputs may be any that keep to these rules, and one draw needn't show every extreme that they name: `coverage`: within the rows of one device (aligned blocks of 16 rows) no tile is named more than 2 times; in every block one tile is named exactly 2 times.
All inputs are finite; a program needn't handle non-finite values.
Results may differ from the reference program's by a relative error of at most 0.012.
Values may be sent and summed in bfloat16 or wider, within the bound.
A program may use at most 128 MiB of HBM per device.

```python
import math
import jax
import jax.numpy as jnp
from jax import lax

PULSES_DEV = 128
RANGE = 16384
CHIRP = 512
BEAMS = 128
BAND = 8
SECTIONS = 4
TB = 32
TR = 256
CAP = 2
SUBAPS = 16
PULSES = 2048
RBINS = 8192
RBLOCKS = 2
RBINS_DEV = 4096
TILES = 32
SLOTS = 16
SLOTS_ALL = 512
N_RNG = 2


def draw_coverage(key, part):
    hottest = jax.random.randint(jax.random.fold_in(key, 11), (), 0, TILES)
    popularity = jax.random.randint(jax.random.fold_in(key, 12), (TILES,), 0, 4)
    tile_ids = jnp.arange(TILES).astype(jnp.int32)

    def one_device(device_key):
        first_key, second_key, third_key = jax.random.split(device_key, 3)
        shuffled = jax.random.permutation(first_key, TILES).astype(jnp.int32)
        scores = (popularity * (TILES // 2) + shuffled) * TILES + shuffled
        scores = jnp.where(tile_ids == hottest, -1, scores)
        unused, picked = lax.top_k(scores, SLOTS - CAP)
        picked = picked.astype(jnp.int32)
        repeat_flag = jax.random.randint(second_key, (), 0, 2)
        last_entry = jnp.where(repeat_flag == 1, picked[0], picked[SLOTS - CAP - 1])
        picked = jnp.concatenate([picked[:SLOTS - CAP - 1], last_entry[None]])
        entries = jnp.concatenate([jnp.full((CAP,), hottest, jnp.int32), picked])
        ordering = jax.random.permutation(third_key, SLOTS)
        return entries[ordering]
    device_keys = jax.random.split(jax.random.fold_in(key, 13), TILES)
    return jax.vmap(one_device)(device_keys).reshape(SLOTS_ALL, 1).astype(jnp.int32)


def with_ends(values, stream_key, smallest, largest):
    shape = values.shape
    spot = [jax.random.randint(jax.random.fold_in(stream_key, axis), (), 0, shape[axis]) for axis in range(len(shape))]
    values = values.at[tuple(spot)].set(smallest)
    longest = shape.index(max(shape))
    spot[longest] = (spot[longest] + 1) % shape[longest]
    return values.at[tuple(spot)].set(largest)


def level_of(key, extent, cuts, least, top_value):
    gain = 1.0
    for axis_at, blocks in cuts:
        heights = jax.random.uniform(jax.random.fold_in(jax.random.fold_in(key, 6), axis_at), (blocks,), jnp.float32, least / len(cuts), top_value / len(cuts))
        gain = gain * jnp.repeat(jnp.exp(heights), extent[axis_at] // blocks).reshape((-1,) + (1,) * (len(extent) - 1 - axis_at))
    return gain


def gaussian(rng, shape, deviation, most, shards=(), kind=jnp.bfloat16):
    loudness = level_of(rng, shape, shards, -0.22, 0.18) if shards else 1.0
    result = jax.random.normal(rng, shape, jnp.float32) * deviation * loudness
    return jnp.minimum(jnp.maximum(result, -most), most).astype(kind)


def setup_inputs(seed: int = 0) -> dict:
    keys = jax.random.split(jax.random.key(seed), 10)
    return {
        "raw_echoes": gaussian(keys[0], (PULSES, 2, RANGE), 1.0, 6.0, ((0, 16), (2, 2))),
        "chirp_replica": gaussian(keys[1], (2, CHIRP), (2 * CHIRP) ** -0.5, 0.1875),
        "steering": gaussian(keys[2], (SUBAPS, 2, BEAMS, PULSES_DEV), (2 * PULSES_DEV) ** -0.5, 0.375, ((0, 16),)),
        "band_start": with_ends(jax.random.randint(keys[3], (SECTIONS, SUBAPS, 2, BEAMS), 0, BEAMS - BAND + 1), jax.random.fold_in(keys[3], 1), 0, BEAMS - BAND).astype(jnp.int32),
        "band_coef": gaussian(keys[4], (SECTIONS, SUBAPS, 2, 2, BAND, BEAMS), (4 * BAND) ** -0.5, 1.0, ((1, 16),)),
        "phase_rate": jnp.clip(jax.random.uniform(keys[5], (SECTIONS, SUBAPS, BEAMS), jnp.float32, -8.0, 8.0) * level_of(keys[5], (SECTIONS, SUBAPS, BEAMS), ((1, 16),), -0.4, 0.0), -8.0, 8.0),
        "range_map": gaussian(keys[6], (2, RBINS, TR), (2 * RBINS // N_RNG) ** -0.5, 0.0625, ((1, 2),)),
        "slot_maps": gaussian(keys[7], (SLOTS_ALL, 2, TB, BEAMS), (2 * BEAMS * SLOTS) ** -0.5, 0.09375, ((0, 32),)),
        "coverage": draw_coverage(jax.random.fold_in(keys[9], 71), 0),
    }


def toeplitz_taps(replica):
    quarter = CHIRP // 4
    window_width = 6 * quarter
    positions = jnp.arange(window_width).astype(jnp.int32)[:, None] - 2 * jnp.arange(quarter).astype(jnp.int32)[None, :]
    inside = (positions >= 0) & (positions < CHIRP)
    clipped = jnp.clip(positions, 0, CHIRP - 1)
    values = replica.astype(jnp.float32)[:, clipped]
    return jnp.where(inside[None], values, jnp.float32(0.0))


def compress(pulse_block, toeplitz):
    quarter = CHIRP // 4
    stride = 2 * quarter
    window_count = RANGE // stride
    data = pulse_block.astype(jnp.float32)
    pulses = data.shape[0]
    padded = jnp.concatenate([data, jnp.zeros((pulses, 2, CHIRP), jnp.float32)], axis=2)
    blocks = padded.reshape(pulses, 2, window_count + 2, stride)
    windows = jnp.concatenate([blocks[:, :, :window_count], blocks[:, :, 1:window_count + 1], blocks[:, :, 2:]], axis=3)
    products = jnp.einsum("pcnw,ewq->pcenq", windows, toeplitz)
    real_part = products[:, 0, 0] + products[:, 1, 1]
    imag_part = products[:, 1, 0] - products[:, 0, 1]
    return jnp.stack([real_part, imag_part], axis=1).reshape(pulses, 2, RBINS).astype(jnp.bfloat16)


def project(items):
    steer, pulse_rows = items
    products = jnp.einsum("cbp,pdr->cdbr", steer.astype(jnp.float32), pulse_rows.astype(jnp.float32))
    return jnp.stack([products[0, 0] - products[1, 1], products[0, 1] + products[1, 0]]).astype(jnp.bfloat16)


def band_apply(field, starts, coefs):
    rows = starts[:, None] + jnp.arange(BAND).astype(jnp.int32)[None, :]
    picked = field.astype(jnp.float32)[:, rows, :]
    coef_real = jnp.transpose(coefs[0].astype(jnp.float32))[:, :, None]
    coef_imag = jnp.transpose(coefs[1].astype(jnp.float32))[:, :, None]
    real_part = jnp.sum(coef_real * picked[0] - coef_imag * picked[1], axis=1)
    imag_part = jnp.sum(coef_real * picked[1] + coef_imag * picked[0], axis=1)
    return real_part, imag_part


def merge(items):
    own_image, partner_image, starts, coefs, rates = items
    own_real, own_imag = band_apply(own_image, starts[0], coefs[0])
    part_real, part_imag = band_apply(partner_image, starts[1], coefs[1])
    bins = jnp.arange(RBINS).astype(jnp.float32)
    angle = (rates.astype(jnp.float32)[:, None] * bins[None, :]) * (2.0 * math.pi / RBINS_DEV)
    cosine = jnp.cos(angle)
    sine = jnp.sin(angle)
    turned_real = part_real * cosine - part_imag * sine
    turned_imag = part_real * sine + part_imag * cosine
    return jnp.stack([own_real + turned_real, own_imag + turned_imag]).astype(jnp.bfloat16)


def reference(raw_echoes, chirp_replica, steering, band_start, band_coef, phase_rate, range_map, slot_maps, coverage):
    toeplitz = toeplitz_taps(chirp_replica)
    compressed = lax.map(lambda pulse_block: compress(pulse_block, toeplitz), raw_echoes.reshape(SUBAPS, PULSES_DEV, 2, RANGE))
    polar = lax.map(project, (steering, compressed))
    for section_bit in range(SECTIONS):
        group = 2 ** section_bit
        partner = polar.reshape(SUBAPS // (2 * group), 2, group, 2, BEAMS, RBINS)[:, ::-1].reshape(SUBAPS, 2, BEAMS, RBINS)
        polar = lax.map(merge, (polar, partner, band_start[section_bit], band_coef[section_bit], phase_rate[section_bit]))
    maps_float = range_map.astype(jnp.float32).reshape(2, RBLOCKS, RBINS_DEV, TR)

    def basis_of(polar_image):
        pieces = polar_image.astype(jnp.float32).reshape(2, BEAMS, RBLOCKS, RBINS_DEV)
        products = jnp.einsum("cbhr,dhrt->cdhbt", pieces, maps_float)
        stacked = jnp.stack([products[0, 0] - products[1, 1], products[0, 1] + products[1, 0]])
        return jnp.transpose(stacked, (1, 0, 2, 3)).astype(jnp.bfloat16)

    tile_basis = lax.map(basis_of, polar).reshape(TILES, 2, BEAMS, TR)

    def accumulate(total, items):
        basis, maps, targets = items
        products = jnp.einsum("kcab,dbt->kcdat", maps.astype(jnp.float32), basis.astype(jnp.float32))
        parts = jnp.stack([products[:, 0, 0] - products[:, 1, 1], products[:, 0, 1] + products[:, 1, 0]], axis=1).reshape(SLOTS, 2 * TB * TR)
        select = (jnp.arange(TILES).astype(jnp.int32)[:, None] == targets[None, :]).astype(jnp.float32)
        return total + jnp.dot(select, parts, precision=lax.Precision.HIGHEST, preferred_element_type=jnp.float32), None

    initial = jnp.zeros((TILES, 2 * TB * TR), jnp.float32)
    total, unused = lax.scan(accumulate, initial, (tile_basis, slot_maps.reshape(TILES, SLOTS, 2, TB, BEAMS), coverage.reshape(TILES, SLOTS)))
    return total.reshape(TILES, 2, TB, TR)
```

```python
import functools
import math

import jax
import jax.numpy as jnp
from jax import lax
from jax.experimental import pallas as pl
from jax.experimental.pallas import tpu as pltpu
from jax.sharding import PartitionSpec as P

LANES = 128
ROWS = 24
F32 = jnp.float32
BF16 = jnp.bfloat16
MESH = pl.DeviceIdType.MESH
MIB = 1024 * 1024


def mm(a, b):
    return jnp.dot(a, b, preferred_element_type=F32)


def mm_first(a, b):
    return lax.dot_general(a, b, (((0,), (0,)), ((), ())), preferred_element_type=F32)


def mm_last(a, b):
    return lax.dot_general(a, b, (((1,), (1,)), ((), ())), preferred_element_type=F32)


def top_bit(e):
    return e.bit_length() - 1


def low_bit(e):
    return (e & -e).bit_length() - 1


def node_order(sections):
    return sorted(range(1, 2**sections), key=lambda e: (low_bit(e), e))


def flipped(index, mask):
    out = index
    for k in range(mask.bit_length()):
        if mask >> k & 1:
            out = out + 2**k * (1 - 2 * lax.rem(lax.div(index, 2**k), 2))
    return out


def meet(devices):
    barrier = pltpu.get_barrier_semaphore()
    for device in devices:
        pl.semaphore_signal(barrier, inc=1, device_id=device, device_id_type=MESH)
    pl.semaphore_wait(barrier, len(devices))


def front_kernel(
    sections,
    steer_ref,
    chirp_ref,
    raw_ref,
    turns_ref,
    owns_ref,
    polar_ref,
    turns_all,
    owns_all,
    field,
    halo,
    steer_out,
    taps,
    halo_sems,
    turn_send,
    turn_recv,
    own_send,
    own_recv,
):
    sub, rng = lax.axis_index("sub"), lax.axis_index("rng")
    nodes = 2**sections
    order = node_order(sections)
    rows, length = raw_ref.shape
    reach = halo.shape[1]
    beams = steer_ref.shape[2]
    quarter = reach // 4
    stride = 2 * quarter
    width = 6 * quarter
    partner = (sub, 1 - rng)
    meet([partner] + [(flipped(sub, e), rng) for e in range(1, nodes)])
    copies = []
    halo_copy = pltpu.make_async_remote_copy(
        src_ref=raw_ref.at[:, pl.ds(0, reach)],
        dst_ref=halo,
        send_sem=halo_sems.at[0],
        recv_sem=halo_sems.at[1],
        device_id=partner,
        device_id_type=MESH,
    )
    halo_copy.start()
    for i, e in enumerate(order):
        top = top_bit(e)
        there = (flipped(sub, e), rng)
        copies.append(
            pltpu.make_async_remote_copy(
                src_ref=turns_ref.at[top],
                dst_ref=turns_all.at[i],
                send_sem=turn_send.at[i],
                recv_sem=turn_recv.at[i],
                device_id=there,
                device_id_type=MESH,
            )
        )
        if top + 1 < sections:
            kept = pl.ds(top + 1, sections - top - 1)
            copies.append(
                pltpu.make_async_remote_copy(
                    src_ref=owns_ref.at[kept],
                    dst_ref=owns_all.at[e, kept],
                    send_sem=own_send.at[e],
                    recv_sem=own_recv.at[e],
                    device_id=there,
                    device_id_type=MESH,
                )
            )
    for copy in copies:
        copy.start()
    owns_all[0] = owns_ref[...]

    real, imag = steer_ref[0, 0], steer_ref[0, 1]
    apart = jnp.concatenate(
        [jnp.concatenate([real, -imag], axis=1), jnp.concatenate([imag, real], axis=1)], axis=0
    )
    pulses = rows // 2
    source = lax.broadcasted_iota(jnp.int32, (rows, rows), 0)
    target = lax.broadcasted_iota(jnp.int32, (rows, rows), 1)
    place = jnp.where(source < pulses, 2 * source, 2 * (source - pulses) + 1)
    weave = (place == target).astype(F32).astype(BF16)
    steer_out[...] = mm(apart, weave).astype(BF16)
    for c in range(2):
        line = chirp_ref[c : c + 1, :].astype(F32)
        line = jnp.concatenate([line, jnp.zeros((1, width - reach), F32)], axis=1)
        tall = jnp.broadcast_to(line, (quarter, width))
        rolled = pltpu.roll(tall, 0, 1, stride=2, stride_axis=0)
        taps[c * quarter : (c + 1) * quarter, :] = rolled.astype(BF16)

    chunk = 4 * stride
    steer = steer_out[...]

    def steered(k, carry):
        at = pl.ds(pl.multiple_of(k * chunk, chunk), chunk)
        field[:, at] = mm(steer, raw_ref[:, at]).astype(BF16)
        return carry

    lax.fori_loop(0, length // chunk, steered, 0, unroll=True)

    def window(n, carry):
        at = pl.ds(pl.multiple_of(n * stride, stride), width)
        both = mm_last(taps[...], field[:, at])
        here = pl.ds(pl.multiple_of(n * quarter, quarter), quarter)
        polar_ref[here, :beams] = (both[:quarter, :beams] + both[quarter:, beams:]).astype(BF16)
        polar_ref[here, beams:] = (both[:quarter, beams:] - both[quarter:, :beams]).astype(BF16)
        return carry

    count = length // stride
    inner = count - 2
    lax.fori_loop(0, inner, window, 0, unroll=True)
    halo_copy.wait()
    tail = mm(steer, halo[...])
    tail = jnp.where(rng == 0, tail, jnp.zeros_like(tail))
    field[:, length:] = tail.astype(BF16)
    for n in range(inner, count):
        window(n, 0)
    for copy in copies:
        copy.wait()


def front(steering, chirp, raw, turns, owns, sections):
    rows, length = raw.shape
    reach = chirp.shape[1]
    nodes = 2**sections
    beams = steering.shape[2]
    vmem = pl.BlockSpec(memory_space=pltpu.VMEM)
    dma = pltpu.SemaphoreType.DMA
    return pl.pallas_call(
        functools.partial(front_kernel, sections),
        in_specs=[vmem] * 5,
        out_specs=[vmem] * 3,
        out_shape=[
            jax.ShapeDtypeStruct((length // 2, 2 * beams), BF16),
            jax.ShapeDtypeStruct((nodes - 1, ROWS, beams), F32),
            jax.ShapeDtypeStruct((nodes // 2, sections, ROWS, beams), F32),
        ],
        scratch_shapes=[
            pltpu.VMEM((2 * beams, length + reach), BF16),
            pltpu.VMEM((rows, reach), BF16),
            pltpu.VMEM((2 * beams, rows), BF16),
            pltpu.VMEM((reach // 2, 6 * (reach // 4)), BF16),
            dma((2,)),
            dma((nodes - 1,)),
            dma((nodes - 1,)),
            dma((nodes // 2,)),
            dma((nodes // 2,)),
        ],
        compiler_params=pltpu.CompilerParams(
            vmem_limit_bytes=32 * MIB, collective_id=0, has_side_effects=True
        ),
        cost_estimate=pl.CostEstimate(flops=4 * 10**9, bytes_accessed=7 * 10**6, transcendentals=0),
        name="front",
    )(steering, chirp, raw, turns, owns)


def turned(turns):
    whole = turns - lax.round(turns, lax.RoundingMethod.TO_NEAREST_EVEN)
    y = whole * math.pi
    y2 = y * y
    sine = jnp.full_like(y, -1.0 / math.factorial(11))
    for k in (9, 7, 5, 3, 1):
        sine = sine * y2 + (-1.0) ** (k // 2) / math.factorial(k)
    sine = sine * y
    cosine = jnp.full_like(y, 1.0 / math.factorial(12))
    for k in (10, 8, 6, 4, 2, 0):
        cosine = cosine * y2 + (-1.0) ** (k // 2) / math.factorial(k)
    return 1.0 - 2.0 * sine * sine, 2.0 * sine * cosine


def matrices_kernel(
    sections,
    taps,
    bins,
    place_ref,
    block_ref,
    turns_ref,
    owns_ref,
    turn_ref,
    chain_ref,
    fine_ref,
    coarse_ref,
    slot_ref,
    built,
):
    beams = turns_ref.shape[2]
    nodes = 2**sections
    order = node_order(sections)
    rows = lax.broadcasted_iota(jnp.int32, (beams, beams), 0).astype(F32)

    def complex_of(data):
        offset = rows - data[2 * taps : 2 * taps + 1, :]
        real = jnp.zeros((beams, beams), F32)
        imag = jnp.zeros((beams, beams), F32)
        for t in range(taps):
            hit = offset == t
            real = jnp.where(hit, data[t : t + 1, :], real)
            imag = jnp.where(hit, data[taps + t : taps + t + 1, :], imag)
        upper = jnp.concatenate([real, imag], axis=1)
        lower = jnp.concatenate([-imag, real], axis=1)
        return jnp.concatenate([upper, lower], axis=0).astype(BF16)

    for e in range(nodes):
        chain = None
        for s in range(top_bit(e) + 1, sections):
            child = e | 2**s
            partner = complex_of(turns_ref[order.index(child)])
            turn_ref[order.index(child)] = (
                partner if chain is None else mm(chain, partner).astype(BF16)
            )
            own = complex_of(owns_ref[e, s])
            chain = own if chain is None else mm(chain, own).astype(BF16)
        if chain is not None:
            chain_ref[e] = chain

    lane = lax.broadcasted_iota(jnp.int32, (LANES, beams), 0).astype(F32)
    blocks = coarse_ref.shape[2]
    first = lax.broadcasted_iota(jnp.int32, (blocks, beams), 0) * LANES + block_ref[0] * bins
    first = first.astype(F32)
    for i in range(nodes - 1):
        rate = turns_ref[i, 2 * taps + 1 : 2 * taps + 2, :]
        fine_ref[i, 0], fine_ref[i, 1] = turned(rate * lane * (1.0 / bins))
        coarse_ref[i, 0], coarse_ref[i, 1] = turned(rate * first * (1.0 / bins))

    slots = place_ref.shape[0]

    def clear(n, carry):
        slot_ref[n] = slots
        return carry

    def enter(k, carry):
        at = 2 * place_ref[k]
        at = at + (slot_ref[at] != slots).astype(jnp.int32)
        slot_ref[at] = k
        return carry

    lax.fori_loop(0, slot_ref.shape[0], clear, 0)
    lax.fori_loop(0, slots, enter, 0)


def matrices(place, block, turns, owns, sections, taps, bins, tiles):
    nodes = 2**sections
    beams = turns.shape[2]
    vmem = pl.BlockSpec(memory_space=pltpu.VMEM)
    smem = pl.BlockSpec(memory_space=pltpu.SMEM)
    pair = 2 * beams
    return pl.pallas_call(
        functools.partial(matrices_kernel, sections, taps, bins),
        in_specs=[smem, smem, vmem, vmem],
        out_specs=[vmem, vmem, vmem, vmem, smem],
        out_shape=[
            jax.ShapeDtypeStruct((nodes - 1, pair, pair), BF16),
            jax.ShapeDtypeStruct((nodes // 2, pair, pair), BF16),
            jax.ShapeDtypeStruct((nodes - 1, 2, LANES, beams), F32),
            jax.ShapeDtypeStruct((nodes - 1, 2, bins // LANES, beams), F32),
            jax.ShapeDtypeStruct((2 * tiles,), jnp.int32),
        ],
        scratch_shapes=[pltpu.VMEM((8, LANES), F32)],
        compiler_params=pltpu.CompilerParams(vmem_limit_bytes=32 * MIB),
        cost_estimate=pl.CostEstimate(flops=5 * 10**9, bytes_accessed=5 * 10**6, transcendentals=0),
        name="matrices",
    )(place, block, turns, owns)


def tree_kernel(
    sections,
    slot_ref,
    polar_ref,
    map_hbm,
    turn_ref,
    chain_ref,
    fine_ref,
    coarse_ref,
    maps_ref,
    out_ref,
    fields,
    leaves,
    range_map,
    sent,
    got,
    parts,
    total,
    tiles_sent,
    tiles_got,
    map_sem,
    basis_send,
    basis_recv,
    tile_send,
    tile_recv,
):
    sub, rng = lax.axis_index("sub"), lax.axis_index("rng")
    nodes = 2**sections
    order = node_order(sections)
    bins, pair = polar_ref.shape
    beams = pair // 2
    tiles = tiles_got.shape[0]
    levels = top_bit(tiles)
    slots, _, tile_rows, _ = maps_ref.shape
    chunk = 512
    fetch = pltpu.make_async_copy(map_hbm, range_map, map_sem)
    fetch.start()
    meet([(sub, 1 - rng)] + [(flipped(sub, 2**k), rng) for k in range(max(sections, levels - 1))])

    def merge(i, source, target):
        def step(c, carry):
            base = pl.multiple_of(c * chunk, chunk)
            value = mm(source[pl.ds(base, chunk), :], turn_ref[i])
            fine_cos, fine_sin = fine_ref[i, 0], fine_ref[i, 1]
            for j in range(chunk // LANES):
                at = pl.ds(c * (chunk // LANES) + j, 1)
                cos, sin = coarse_ref[i, 0, at, :], coarse_ref[i, 1, at, :]
                cosine = fine_cos * cos - fine_sin * sin
                sine = fine_cos * sin + fine_sin * cos
                here = value[j * LANES : (j + 1) * LANES]
                real, imag = here[:, :beams], here[:, beams:]
                both = jnp.concatenate(
                    [real * cosine - imag * sine, real * sine + imag * cosine], axis=1
                )
                target[pl.ds(pl.multiple_of(base + j * LANES, LANES), LANES), :] = both.astype(BF16)
            return carry

        lax.fori_loop(0, bins // chunk, step, 0, unroll=True)

    def project(e, field):
        by_real = mm_first(field[...], range_map[0])
        by_imag = mm_first(field[...], range_map[1])
        basis = jnp.concatenate(
            [by_real[:beams] - by_imag[beams:], by_imag[:beams] + by_real[beams:]], axis=0
        )
        if e < nodes // 2:
            basis = mm_first(chain_ref[e], basis.astype(BF16))
        return basis

    def place_of(e):
        if e == 0:
            return polar_ref
        if e < nodes // 2:
            return fields.at[e - 1]
        return leaves.at[order.index(e) % leaves.shape[0]]

    def message(e):
        i = order.index(e)
        return pltpu.make_async_remote_copy(
            src_ref=sent.at[i],
            dst_ref=got.at[i],
            send_sem=basis_send.at[i],
            recv_sem=basis_recv.at[i],
            device_id=(flipped(sub, 2 ** low_bit(e)), rng),
            device_id_type=MESH,
        )

    def gathered(e, basis):
        for k in range(low_bit(e) if e else sections):
            other = e | 2**k
            message(other).wait_recv()
            basis = basis + got[order.index(other)].astype(F32)
        return basis

    for i, e in enumerate(order):
        field = place_of(e)
        merge(i, place_of(e ^ 2 ** top_bit(e)), field)
        if i == 0:
            fetch.wait()
        basis = gathered(e, project(e, field))
        sent[i] = basis.astype(BF16)
        message(e).start()

    real = maps_ref[:, 0].reshape(slots * tile_rows, beams)
    imag = maps_ref[:, 1].reshape(slots * tile_rows, beams)
    basis = gathered(0, project(0, polar_ref)).astype(BF16)
    shape = (slots, tile_rows, basis.shape[1])
    parts[:slots, 0] = mm(jnp.concatenate([real, -imag], axis=1), basis).reshape(shape)
    parts[:slots, 1] = mm(jnp.concatenate([imag, real], axis=1), basis).reshape(shape)
    parts[slots] = jnp.zeros_like(parts[slots])

    def exchange(k):
        half = tiles >> (k + 1)
        there = (flipped(sub, 2 ** (k - 1)), rng) if k else (sub, 1 - rng)
        return pltpu.make_async_remote_copy(
            src_ref=tiles_sent.at[pl.ds(half, half)],
            dst_ref=tiles_got.at[pl.ds(half, half)],
            send_sem=tile_send.at[k],
            recv_sem=tile_recv.at[k],
            device_id=there,
            device_id_type=MESH,
        )

    half = tiles // 2

    def outer(t, carry):
        tiles_sent[t] = (parts[slot_ref[2 * t]] + parts[slot_ref[2 * t + 1]]).astype(BF16)
        return carry

    def inner(t, carry):
        total[t] = parts[slot_ref[2 * t]] + parts[slot_ref[2 * t + 1]]
        return carry

    lax.fori_loop(half, tiles, outer, 0)
    exchange(0).start()
    lax.fori_loop(0, half, inner, 0)
    for k in range(levels):
        half = tiles >> (k + 1)
        exchange(k).wait_recv()
        if half > 1:
            quarter = half // 2

            def upper(t, carry):
                tiles_sent[t] = (total[t] + tiles_got[half + t].astype(F32)).astype(BF16)
                return carry

            def lower(t, carry):
                total[t] = total[t] + tiles_got[half + t].astype(F32)
                return carry

            lax.fori_loop(quarter, half, upper, 0)
            exchange(k + 1).start()
            lax.fori_loop(0, quarter, lower, 0)
        else:
            out_ref[0] = total[0] + tiles_got[1].astype(F32)
    for e in order:
        message(e).wait_send()
    for k in range(levels):
        exchange(k).wait_send()


def tree(slot_of, polar, range_map, turn, chain, fine, coarse, maps, sections, tiles):
    bins, pair = polar.shape
    nodes = 2**sections
    cols = range_map.shape[2]
    slots, _, tile_rows, _ = maps.shape
    levels = top_bit(tiles)
    vmem = pl.BlockSpec(memory_space=pltpu.VMEM)
    dma = pltpu.SemaphoreType.DMA
    tile = (2, tile_rows, cols)
    return pl.pallas_call(
        functools.partial(tree_kernel, sections),
        in_specs=[pl.BlockSpec(memory_space=pltpu.SMEM), vmem, pl.BlockSpec(memory_space=pl.ANY)]
        + [vmem] * 5,
        out_specs=vmem,
        out_shape=jax.ShapeDtypeStruct((1,) + tile, F32),
        scratch_shapes=[
            pltpu.VMEM((nodes // 2 - 1, bins, pair), BF16),
            pltpu.VMEM((2, bins, pair), BF16),
            pltpu.VMEM(range_map.shape, BF16),
            pltpu.VMEM((nodes - 1, pair, cols), BF16),
            pltpu.VMEM((nodes - 1, pair, cols), BF16),
            pltpu.VMEM((slots + 1,) + tile, F32),
            pltpu.VMEM((tiles // 2,) + tile, F32),
            pltpu.VMEM((tiles,) + tile, BF16),
            pltpu.VMEM((tiles,) + tile, BF16),
            dma,
            dma((nodes - 1,)),
            dma((nodes - 1,)),
            dma((levels,)),
            dma((levels,)),
        ],
        compiler_params=pltpu.CompilerParams(
            vmem_limit_bytes=60 * MIB, collective_id=1, has_side_effects=True
        ),
        cost_estimate=pl.CostEstimate(flops=26 * 10**9, bytes_accessed=12 * 10**6, transcendentals=0),
        name="tree",
    )(slot_of, polar, range_map, turn, chain, fine, coarse, maps)


def shards(
    raw_echoes,
    chirp_replica,
    steering,
    band_start,
    band_coef,
    phase_rate,
    range_map,
    slot_maps,
    coverage,
):
    pulses, _, range_len = raw_echoes.shape
    sections, _, _, _, band, beams = band_coef.shape
    cores = lax.axis_size("rng")
    tiles = lax.axis_size("sub") * cores
    bins = range_len // 2

    packed = jnp.concatenate(
        [
            band_coef[:, 0].astype(F32).reshape(sections, 2, 2 * band, beams),
            band_start[:, 0].astype(F32)[:, :, None],
            jnp.broadcast_to(phase_rate[:, 0][:, None, None], (sections, 2, 1, beams)),
            jnp.zeros((sections, 2, ROWS - 2 * band - 2, beams), F32),
        ],
        axis=2,
    )
    raw = raw_echoes.reshape(2 * pulses, range_len)
    me = lax.axis_index("sub") * cores + lax.axis_index("rng")
    levels = top_bit(tiles)
    away = coverage[:, 0] ^ me
    place = sum(((away >> k) & 1) << (levels - 1 - k) for k in range(levels))
    polar, turns, owns = front(
        steering, chirp_replica, raw, packed[:, 1], packed[:, 0], sections
    )
    block = lax.axis_index("rng").reshape(1)
    turn, chain, fine, coarse, slot_of = matrices(
        place, block, turns, owns, sections, band, bins, tiles
    )
    return tree(slot_of, polar, range_map, turn, chain, fine, coarse, slot_maps, sections, tiles)


def solution(mesh):
    in_specs = (
        P("sub", None, "rng"),
        P(),
        P("sub", None, None, None),
        P(None, "sub", None, None),
        P(None, "sub", None, None, None, None),
        P(None, "sub", None),
        P(None, "rng", None),
        P(("sub", "rng"), None, None, None),
        P(("sub", "rng"), None),
    )
    out_specs = P(("sub", "rng"), None, None, None)
    return jax.shard_map(shards, mesh=mesh, in_specs=in_specs, out_specs=out_specs, check_vma=False)
```

```python
import functools
import math

import jax
import jax.numpy as jnp
from jax import lax
from jax.experimental import pallas as pl
from jax.experimental.pallas import tpu as pltpu
from jax.sharding import PartitionSpec as P

LANES = 128
ROWS = 24
F32 = jnp.float32
BF16 = jnp.bfloat16
MESH = pl.DeviceIdType.MESH
MIB = 1024 * 1024


def mm(a, b):
    return jnp.dot(a, b, preferred_element_type=F32)


def mm_first(a, b):
    return lax.dot_general(a, b, (((0,), (0,)), ((), ())), preferred_element_type=F32)


def mm_last(a, b):
    return lax.dot_general(a, b, (((1,), (1,)), ((), ())), preferred_element_type=F32)


def top_bit(e):
    return e.bit_length() - 1


def low_bit(e):
    return (e & -e).bit_length() - 1


def node_order(sections):
    return sorted(range(1, 2**sections), key=lambda e: (low_bit(e), e))


def flipped(index, mask):
    out = index
    for k in range(mask.bit_length()):
        if mask >> k & 1:
            out = out + 2**k * (1 - 2 * lax.rem(lax.div(index, 2**k), 2))
    return out


def meet(devices):
    barrier = pltpu.get_barrier_semaphore()
    for device in devices:
        pl.semaphore_signal(barrier, inc=1, device_id=device, device_id_type=MESH)
    pl.semaphore_wait(barrier, len(devices))


def front_kernel(
    sections,
    steer_ref,
    chirp_ref,
    raw_ref,
    turns_ref,
    owns_ref,
    polar_ref,
    turns_all,
    owns_all,
    field,
    halo,
    steer_out,
    taps,
    halo_sems,
    turn_send,
    turn_recv,
    own_send,
    own_recv,
):
    sub, rng = lax.axis_index("sub"), lax.axis_index("rng")
    nodes = 2**sections
    order = node_order(sections)
    rows, length = raw_ref.shape
    reach = halo.shape[1]
    beams = steer_ref.shape[2]
    quarter = reach // 4
    stride = 2 * quarter
    width = 6 * quarter
    partner = (sub, 1 - rng)
    meet([partner] + [(flipped(sub, e), rng) for e in range(1, nodes)])
    copies = []
    halo_copy = pltpu.make_async_remote_copy(
        src_ref=raw_ref.at[:, pl.ds(0, reach)],
        dst_ref=halo,
        send_sem=halo_sems.at[0],
        recv_sem=halo_sems.at[1],
        device_id=partner,
        device_id_type=MESH,
    )
    halo_copy.start()
    for i, e in enumerate(order):
        top = top_bit(e)
        there = (flipped(sub, e), rng)
        copies.append(
            pltpu.make_async_remote_copy(
                src_ref=turns_ref.at[top],
                dst_ref=turns_all.at[i],
                send_sem=turn_send.at[i],
                recv_sem=turn_recv.at[i],
                device_id=there,
                device_id_type=MESH,
            )
        )
        if top + 1 < sections:
            kept = pl.ds(top + 1, sections - top - 1)
            copies.append(
                pltpu.make_async_remote_copy(
                    src_ref=owns_ref.at[kept],
                    dst_ref=owns_all.at[e, kept],
                    send_sem=own_send.at[e],
                    recv_sem=own_recv.at[e],
                    device_id=there,
                    device_id_type=MESH,
                )
            )
    for copy in copies:
        copy.start()
    owns_all[0] = owns_ref[...]

    real, imag = steer_ref[0, 0], steer_ref[0, 1]
    apart = jnp.concatenate(
        [jnp.concatenate([real, -imag], axis=1), jnp.concatenate([imag, real], axis=1)], axis=0
    )
    pulses = rows // 2
    source = lax.broadcasted_iota(jnp.int32, (rows, rows), 0)
    target = lax.broadcasted_iota(jnp.int32, (rows, rows), 1)
    place = jnp.where(source < pulses, 2 * source, 2 * (source - pulses) + 1)
    weave = (place == target).astype(F32).astype(BF16)
    steer_out[...] = mm(apart, weave).astype(BF16)
    for c in range(2):
        line = chirp_ref[c : c + 1, :].astype(F32)
        line = jnp.concatenate([line, jnp.zeros((1, width - reach), F32)], axis=1)
        tall = jnp.broadcast_to(line, (quarter, width))
        rolled = pltpu.roll(tall, 0, 1, stride=2, stride_axis=0)
        taps[c * quarter : (c + 1) * quarter, :] = rolled.astype(BF16)

    chunk = 4 * stride
    steer = steer_out[...]

    def steered(k, carry):
        at = pl.ds(pl.multiple_of(k * chunk, chunk), chunk)
        field[:, at] = mm(steer, raw_ref[:, at]).astype(BF16)
        return carry

    lax.fori_loop(0, length // chunk, steered, 0, unroll=True)

    def window(n, carry):
        at = pl.ds(pl.multiple_of(n * stride, stride), width)
        both = mm_last(taps[...], field[:, at])
        here = pl.ds(pl.multiple_of(n * quarter, quarter), quarter)
        polar_ref[here, :beams] = (both[:quarter, :beams] + both[quarter:, beams:]).astype(BF16)
        polar_ref[here, beams:] = (both[:quarter, beams:] - both[quarter:, :beams]).astype(BF16)
        return carry

    count = length // stride
    inner = count - 2
    lax.fori_loop(0, inner, window, 0, unroll=True)
    halo_copy.wait()
    tail = mm(steer, halo[...])
    tail = jnp.where(rng == 0, tail, jnp.zeros_like(tail))
    field[:, length:] = tail.astype(BF16)
    for n in range(inner, count):
        window(n, 0)
    for copy in copies:
        copy.wait()


def front(steering, chirp, raw, turns, owns, sections):
    rows, length = raw.shape
    reach = chirp.shape[1]
    nodes = 2**sections
    beams = steering.shape[2]
    vmem = pl.BlockSpec(memory_space=pltpu.VMEM)
    dma = pltpu.SemaphoreType.DMA
    return pl.pallas_call(
        functools.partial(front_kernel, sections),
        in_specs=[vmem] * 5,
        out_specs=[vmem] * 3,
        out_shape=[
            jax.ShapeDtypeStruct((length // 2, 2 * beams), BF16),
            jax.ShapeDtypeStruct((nodes - 1, ROWS, beams), F32),
            jax.ShapeDtypeStruct((nodes // 2, sections, ROWS, beams), F32),
        ],
        scratch_shapes=[
            pltpu.VMEM((2 * beams, length + reach), BF16),
            pltpu.VMEM((rows, reach), BF16),
            pltpu.VMEM((2 * beams, rows), BF16),
            pltpu.VMEM((reach // 2, 6 * (reach // 4)), BF16),
            dma((2,)),
            dma((nodes - 1,)),
            dma((nodes - 1,)),
            dma((nodes // 2,)),
            dma((nodes // 2,)),
        ],
        compiler_params=pltpu.CompilerParams(
            vmem_limit_bytes=32 * MIB, collective_id=0, has_side_effects=True
        ),
        cost_estimate=pl.CostEstimate(flops=4 * 10**9, bytes_accessed=7 * 10**6, transcendentals=0),
        name="front",
    )(steering, chirp, raw, turns, owns)


def turned(turns):
    whole = turns - lax.round(turns, lax.RoundingMethod.TO_NEAREST_EVEN)
    y = whole * math.pi
    y2 = y * y
    sine = jnp.full_like(y, -1.0 / math.factorial(11))
    for k in (9, 7, 5, 3, 1):
        sine = sine * y2 + (-1.0) ** (k // 2) / math.factorial(k)
    sine = sine * y
    cosine = jnp.full_like(y, 1.0 / math.factorial(12))
    for k in (10, 8, 6, 4, 2, 0):
        cosine = cosine * y2 + (-1.0) ** (k // 2) / math.factorial(k)
    return 1.0 - 2.0 * sine * sine, 2.0 * sine * cosine


def slots_kernel(tiles, place_ref, slot_ref):
    slots = place_ref.shape[1]

    def clear(n, carry):
        slot_ref[n] = slots
        return carry

    lax.fori_loop(0, slot_ref.shape[0], clear, 0, unroll=8)
    for c in range(place_ref.shape[0]):

        def enter(k, carry):
            at = 2 * (c * tiles + place_ref[c, k])
            at = at + (slot_ref[at] != slots).astype(jnp.int32)
            slot_ref[at] = k
            return carry

        lax.fori_loop(0, slots, enter, 0)


def slots_of(place, tiles):
    smem = pl.BlockSpec(memory_space=pltpu.SMEM)
    return pl.pallas_call(
        functools.partial(slots_kernel, tiles),
        in_specs=[smem],
        out_specs=smem,
        out_shape=jax.ShapeDtypeStruct((place.shape[0] * tiles * 2,), jnp.int32),
        cost_estimate=pl.CostEstimate(flops=1000, bytes_accessed=1000, transcendentals=0),
        name="slots",
    )(place)


def halving_orders(levels):
    first = list(range(levels))
    second = [0, 3, 1, 2] + first[4:] if levels > 3 else first
    return [first, second]


WINDOWS = ((15,), (11, 7), (13, 3), (9, 14), (10, 12), (5, 6), (8, 1), (2, 4))


def tree_kernel(
    sections,
    taps,
    slot_ref,
    polar_ref,
    map_hbm,
    turns_ref,
    owns_ref,
    maps_ref,
    kept_ref,
    came_ref,
    turn_ref,
    chain_ref,
    fine_ref,
    coarse_ref,
    fields,
    leaves,
    range_map,
    sent,
    got,
    parts,
    total,
    tiles_sent,
    tiles_got,
    map_sem,
    basis_send,
    basis_recv,
    tile_send,
    tile_recv,
):
    sub, rng = lax.axis_index("sub"), lax.axis_index("rng")
    nodes = 2**sections
    order = node_order(sections)
    bins, pair = polar_ref.shape
    beams = pair // 2
    tiles = tiles_got.shape[1]
    levels = top_bit(tiles)
    orders = halving_orders(levels)
    slots, _, tile_rows, _ = maps_ref.shape
    chunk = 512
    fetch = pltpu.make_async_copy(map_hbm, range_map, map_sem)
    fetch.start()
    barrier = pltpu.get_barrier_semaphore()
    reach = max(sections, levels - 1)
    friends = [(sub, 1 - rng)] + [(flipped(sub, 2**k), rng) for k in range(reach)]
    for friend in friends:
        pl.semaphore_signal(barrier, inc=1, device_id=friend, device_id_type=MESH)

    depth = lax.broadcasted_iota(jnp.int32, (beams, beams), 0).astype(F32)
    lane = lax.broadcasted_iota(jnp.int32, (LANES, beams), 0).astype(F32)
    blocks = bins // LANES
    first = lax.broadcasted_iota(jnp.int32, (blocks, beams), 0) * LANES + rng * bins
    first = first.astype(F32)

    def complex_of(data):
        offset = depth - data[2 * taps : 2 * taps + 1, :]
        real = jnp.zeros((beams, beams), F32)
        imag = jnp.zeros((beams, beams), F32)
        for t in range(taps):
            hit = offset == t
            real = jnp.where(hit, data[t : t + 1, :], real)
            imag = jnp.where(hit, data[taps + t : taps + t + 1, :], imag)
        upper = jnp.concatenate([real, imag], axis=1)
        lower = jnp.concatenate([-imag, real], axis=1)
        return jnp.concatenate([upper, lower], axis=0).astype(BF16)

    chains = {}

    def chain_of(e, s):
        if (e, s) not in chains:
            at = len(chains)
            own = complex_of(owns_ref[e, s])
            if s > top_bit(e) + 1:
                own = mm(chain_ref[chain_of(e, s - 1)], own).astype(BF16)
                at = len(chains)
            chains[(e, s)] = at
            chain_ref[at] = own
        return chains[(e, s)]

    def prepare(e):
        i, s = order.index(e), top_bit(e)
        parent = e ^ 2**s
        turn = complex_of(turns_ref[i])
        if s > top_bit(parent) + 1:
            turn = mm(chain_ref[chain_of(parent, s - 1)], turn).astype(BF16)
        turn_ref[i] = turn
        rate = turns_ref[i, 2 * taps + 1 : 2 * taps + 2, :]
        fine_ref[i, 0], fine_ref[i, 1] = turned(rate * lane * (1.0 / bins))
        coarse_ref[i, 0], coarse_ref[i, 1] = turned(rate * first * (1.0 / bins))

    def merge(i, source, target):
        def step(c, carry):
            base = pl.multiple_of(c * chunk, chunk)
            value = mm(source[pl.ds(base, chunk), :], turn_ref[i])
            fine_cos, fine_sin = fine_ref[i, 0], fine_ref[i, 1]
            for j in range(chunk // LANES):
                at = pl.ds(c * (chunk // LANES) + j, 1)
                cos, sin = coarse_ref[i, 0, at, :], coarse_ref[i, 1, at, :]
                cosine = fine_cos * cos - fine_sin * sin
                sine = fine_cos * sin + fine_sin * cos
                here = value[j * LANES : (j + 1) * LANES]
                real, imag = here[:, :beams], here[:, beams:]
                both = jnp.concatenate(
                    [real * cosine - imag * sine, real * sine + imag * cosine], axis=1
                )
                target[pl.ds(pl.multiple_of(base + j * LANES, LANES), LANES), :] = both.astype(BF16)
            return carry

        lax.fori_loop(0, bins // chunk, step, 0, unroll=True)

    def project(e, field):
        by_real = mm_first(field[...], range_map[0])
        by_imag = mm_first(field[...], range_map[1])
        basis = jnp.concatenate(
            [by_real[:beams] - by_imag[beams:], by_imag[:beams] + by_real[beams:]], axis=0
        )
        if e < nodes // 2:
            basis = mm_first(chain_ref[chain_of(e, sections - 1)], basis.astype(BF16))
        return basis

    def message(e):
        i = order.index(e)
        return pltpu.make_async_remote_copy(
            src_ref=sent.at[i],
            dst_ref=got.at[i],
            send_sem=basis_send.at[i],
            recv_sem=basis_recv.at[i],
            device_id=(flipped(sub, 2 ** low_bit(e)), rng),
            device_id_type=MESH,
        )

    def needed(e):
        return [e | 2**k for k in range(low_bit(e) if e else sections)]

    def gathered(e, basis):
        for other in needed(e):
            basis = basis + got[order.index(other)].astype(F32)
        return basis

    merged = {0: polar_ref}

    def field_of(e, leaf):
        if e not in merged:
            parent = field_of(e ^ 2 ** top_bit(e), leaf)
            prepare(e)
            target = fields.at[e - 1] if e < nodes // 2 else leaves.at[leaf]
            merge(order.index(e), parent, target)
            merged[e] = target
        return merged[e]

    window_of = {e: w for w, window in enumerate(WINDOWS) for e in window}
    for w, window in enumerate(WINDOWS):
        late = []
        for e in window:
            for other in needed(e):
                if window_of[other] < w - 1:
                    message(other).wait_recv()
                else:
                    late.append(other)
        if w == 0:
            field_of(window[0], 0)
            fetch.wait()
        bases = {}
        for n, e in enumerate(window):
            bases[e] = project(e, field_of(e, n))
            if not late:
                sent[order.index(e)] = gathered(e, bases[e]).astype(BF16)
        for other in late:
            message(other).wait_recv()
        if late:
            for e in window:
                sent[order.index(e)] = gathered(e, bases[e]).astype(BF16)
        if w == 0:
            pl.semaphore_wait(barrier, len(friends))
        for e in window:
            message(e).start()

    real = maps_ref[:, 0].reshape(slots * tile_rows, beams)
    imag = maps_ref[:, 1].reshape(slots * tile_rows, beams)
    basis = project(0, polar_ref)
    for other in needed(0):
        message(other).wait_recv()
    basis = gathered(0, basis).astype(BF16)
    shape = (slots, tile_rows, basis.shape[1])
    parts[0, :slots] = mm(jnp.concatenate([real, -imag], axis=1), basis).reshape(shape)
    parts[1, :slots] = mm(jnp.concatenate([imag, real], axis=1), basis).reshape(shape)
    parts[0, slots] = jnp.zeros(shape[1:], F32)
    parts[1, slots] = jnp.zeros(shape[1:], F32)

    def exchange(c, k):
        half = tiles >> (k + 1)
        bit = orders[c][k]
        there = (flipped(sub, 2 ** (bit - 1)), rng) if bit else (sub, 1 - rng)
        return pltpu.make_async_remote_copy(
            src_ref=tiles_sent.at[c, pl.ds(half, half)],
            dst_ref=tiles_got.at[c, pl.ds(half, half)],
            send_sem=tile_send.at[c, k],
            recv_sem=tile_recv.at[c, k],
            device_id=there,
            device_id_type=MESH,
        )

    def part_of(c, t):
        at = 2 * (c * tiles + t)
        return parts[c, slot_ref[at]] + parts[c, slot_ref[at + 1]]

    half = tiles // 2
    for c in range(2):

        def outer(t, carry):
            tiles_sent[c, t] = part_of(c, t).astype(BF16)
            return carry

        lax.fori_loop(half, tiles, outer, 0, unroll=4)
        exchange(c, 0).start()
    for c in range(2):

        def inner(t, carry):
            total[c, t] = part_of(c, t)
            return carry

        lax.fori_loop(0, half, inner, 0, unroll=4)
    for k in range(levels - 1):
        half = tiles >> (k + 1)
        quarter = half // 2
        for c in range(2):
            exchange(c, k).wait_recv()

            def upper(t, carry):
                value = total[c, t] + tiles_got[c, half + t].astype(F32)
                tiles_sent[c, t] = value.astype(BF16)
                return carry

            lax.fori_loop(quarter, half, upper, 0, unroll=min(4, quarter))
            exchange(c, k + 1).start()
        for c in range(2):

            def lower(t, carry):
                total[c, t] = total[c, t] + tiles_got[c, half + t].astype(F32)
                return carry

            lax.fori_loop(0, quarter, lower, 0, unroll=min(4, quarter))
    for c in range(2):
        exchange(c, levels - 1).wait_recv()
        kept_ref[c] = total[c, 0]
        came_ref[c] = tiles_got[c, 1]
    for e in order:
        message(e).wait_send()
    for c in range(2):
        for k in range(levels):
            exchange(c, k).wait_send()


def tree(slot_of, polar, range_map, turns, owns, maps, sections, taps, tiles):
    bins, pair = polar.shape
    beams = pair // 2
    nodes = 2**sections
    cols = range_map.shape[2]
    slots, _, tile_rows, _ = maps.shape
    levels = top_bit(tiles)
    vmem = pl.BlockSpec(memory_space=pltpu.VMEM)
    dma = pltpu.SemaphoreType.DMA
    tile = (tile_rows, cols)
    return pl.pallas_call(
        functools.partial(tree_kernel, sections, taps),
        in_specs=[pl.BlockSpec(memory_space=pltpu.SMEM), vmem, pl.BlockSpec(memory_space=pl.ANY)]
        + [vmem] * 3,
        out_specs=[vmem, vmem],
        out_shape=[
            jax.ShapeDtypeStruct((2,) + tile, F32),
            jax.ShapeDtypeStruct((2,) + tile, BF16),
        ],
        scratch_shapes=[
            pltpu.VMEM((nodes - 1, pair, pair), BF16),
            pltpu.VMEM((nodes - 1, pair, pair), BF16),
            pltpu.VMEM((nodes - 1, 2, LANES, beams), F32),
            pltpu.VMEM((nodes - 1, 2, bins // LANES, beams), F32),
            pltpu.VMEM((nodes // 2 - 1, bins, pair), BF16),
            pltpu.VMEM((2, bins, pair), BF16),
            pltpu.VMEM(range_map.shape, BF16),
            pltpu.VMEM((nodes - 1, pair, cols), BF16),
            pltpu.VMEM((nodes - 1, pair, cols), BF16),
            pltpu.VMEM((2, slots + 1) + tile, F32),
            pltpu.VMEM((2, tiles // 2) + tile, F32),
            pltpu.VMEM((2, tiles) + tile, BF16),
            pltpu.VMEM((2, tiles) + tile, BF16),
            dma,
            dma((nodes - 1,)),
            dma((nodes - 1,)),
            dma((2, levels)),
            dma((2, levels)),
        ],
        compiler_params=pltpu.CompilerParams(
            vmem_limit_bytes=60 * MIB, collective_id=1, has_side_effects=True
        ),
        cost_estimate=pl.CostEstimate(flops=26 * 10**9, bytes_accessed=12 * 10**6, transcendentals=0),
        name="tree",
    )(slot_of, polar, range_map, turns, owns, maps)


def shards(
    raw_echoes,
    chirp_replica,
    steering,
    band_start,
    band_coef,
    phase_rate,
    range_map,
    slot_maps,
    coverage,
):
    pulses, _, range_len = raw_echoes.shape
    sections, _, _, _, band, beams = band_coef.shape
    cores = lax.axis_size("rng")
    tiles = lax.axis_size("sub") * cores
    bins = range_len // 2

    packed = jnp.concatenate(
        [
            band_coef[:, 0].astype(F32).reshape(sections, 2, 2 * band, beams),
            band_start[:, 0].astype(F32)[:, :, None],
            jnp.broadcast_to(phase_rate[:, 0][:, None, None], (sections, 2, 1, beams)),
            jnp.zeros((sections, 2, ROWS - 2 * band - 2, beams), F32),
        ],
        axis=2,
    )
    raw = raw_echoes.reshape(2 * pulses, range_len)
    me = lax.axis_index("sub") * cores + lax.axis_index("rng")
    levels = top_bit(tiles)
    away = coverage[:, 0] ^ me
    place = jnp.stack(
        [
            sum(((away >> bit) & 1) << (levels - 1 - k) for k, bit in enumerate(order))
            for order in halving_orders(levels)
        ]
    )
    slot_of = slots_of(place, tiles)
    polar, turns, owns = front(
        steering, chirp_replica, raw, packed[:, 1], packed[:, 0], sections
    )
    kept, came = tree(slot_of, polar, range_map, turns, owns, slot_maps, sections, band, tiles)
    return (kept + came.astype(F32))[None]


def solution(mesh):
    in_specs = (
        P("sub", None, "rng"),
        P(),
        P("sub", None, None, None),
        P(None, "sub", None, None),
        P(None, "sub", None, None, None, None),
        P(None, "sub", None),
        P(None, "rng", None),
        P(("sub", "rng"), None, None, None),
        P(("sub", "rng"), None),
    )
    out_specs = P(("sub", "rng"), None, None, None)
    return jax.shard_map(shards, mesh=mesh, in_specs=in_specs, out_specs=out_specs, check_vma=False)
```

```python
import functools
import math

import jax
import jax.numpy as jnp
from jax import lax
from jax.experimental import pallas as pl
from jax.experimental.pallas import tpu as pltpu
from jax.sharding import PartitionSpec as P

LANES = 128
ROWS = 24
F32 = jnp.float32
BF16 = jnp.bfloat16
MESH = pl.DeviceIdType.MESH
MIB = 1024 * 1024


def mm(a, b):
    return jnp.dot(a, b, preferred_element_type=F32)


def mm_first(a, b):
    return lax.dot_general(a, b, (((0,), (0,)), ((), ())), preferred_element_type=F32)


def mm_last(a, b):
    return lax.dot_general(a, b, (((1,), (1,)), ((), ())), preferred_element_type=F32)


def top_bit(e):
    return e.bit_length() - 1


def low_bit(e):
    return (e & -e).bit_length() - 1


def node_order(sections):
    return sorted(range(1, 2**sections), key=lambda e: (low_bit(e), e))


def flipped(index, mask):
    out = index
    for k in range(mask.bit_length()):
        if mask >> k & 1:
            out = out + 2**k * (1 - 2 * lax.rem(lax.div(index, 2**k), 2))
    return out


def meet(devices):
    barrier = pltpu.get_barrier_semaphore()
    for device in devices:
        pl.semaphore_signal(barrier, inc=1, device_id=device, device_id_type=MESH)
    pl.semaphore_wait(barrier, len(devices))


def front_kernel(
    sections,
    steer_ref,
    chirp_ref,
    raw_ref,
    start_ref,
    coef_ref,
    rate_ref,
    polar_ref,
    turns_all,
    owns_all,
    owns_here,
    turns_here,
    field,
    halo,
    steer_out,
    taps,
    halo_sems,
    turn_send,
    turn_recv,
    own_send,
    own_recv,
):
    sub, rng = lax.axis_index("sub"), lax.axis_index("rng")
    nodes = 2**sections
    order = node_order(sections)
    pulses, _, length = raw_ref.shape
    rows = 2 * pulses
    reach = halo.shape[2]
    beams = steer_ref.shape[2]
    band = coef_ref.shape[4]
    quarter = reach // 4
    stride = 2 * quarter
    width = 6 * quarter
    partner = (sub, 1 - rng)
    for s in range(sections):
        for j, packed in enumerate((owns_here, turns_here)):
            for c in range(2):
                packed[s, c * band : (c + 1) * band] = coef_ref[s, 0, j, c].astype(F32)
            packed[s, 2 * band :] = jnp.concatenate(
                [
                    start_ref[s, 0, j : j + 1].astype(F32),
                    rate_ref[s],
                    jnp.zeros((ROWS - 2 * band - 2, beams), F32),
                ],
                axis=0,
            )
    meet([partner] + [(flipped(sub, e), rng) for e in range(1, nodes)])
    copies = []
    halo_copy = pltpu.make_async_remote_copy(
        src_ref=raw_ref.at[:, :, pl.ds(0, reach)],
        dst_ref=halo,
        send_sem=halo_sems.at[0],
        recv_sem=halo_sems.at[1],
        device_id=partner,
        device_id_type=MESH,
    )
    halo_copy.start()
    for i, e in enumerate(order):
        top = top_bit(e)
        there = (flipped(sub, e), rng)
        copies.append(
            pltpu.make_async_remote_copy(
                src_ref=turns_here.at[top],
                dst_ref=turns_all.at[i],
                send_sem=turn_send.at[i],
                recv_sem=turn_recv.at[i],
                device_id=there,
                device_id_type=MESH,
            )
        )
        if top + 1 < sections:
            kept = pl.ds(top + 1, sections - top - 1)
            copies.append(
                pltpu.make_async_remote_copy(
                    src_ref=owns_here.at[kept],
                    dst_ref=owns_all.at[e, kept],
                    send_sem=own_send.at[e],
                    recv_sem=own_recv.at[e],
                    device_id=there,
                    device_id_type=MESH,
                )
            )
    for copy in copies:
        copy.start()
    owns_all[0] = owns_here[...]

    real, imag = steer_ref[0, 0], steer_ref[0, 1]
    apart = jnp.concatenate(
        [jnp.concatenate([real, -imag], axis=1), jnp.concatenate([imag, real], axis=1)], axis=0
    )
    source = lax.broadcasted_iota(jnp.int32, (rows, rows), 0)
    target = lax.broadcasted_iota(jnp.int32, (rows, rows), 1)
    place = jnp.where(source < pulses, 2 * source, 2 * (source - pulses) + 1)
    weave = (place == target).astype(F32).astype(BF16)
    steer_out[...] = mm(apart, weave).astype(BF16)
    for c in range(2):
        line = chirp_ref[c : c + 1, :].astype(F32)
        line = jnp.concatenate([line, jnp.zeros((1, width - reach), F32)], axis=1)
        tall = jnp.broadcast_to(line, (quarter, width))
        rolled = pltpu.roll(tall, 0, 1, stride=2, stride_axis=0)
        taps[c * quarter : (c + 1) * quarter, :] = rolled.astype(BF16)

    chunk = 4 * stride
    steer = steer_out[...]

    for k in range(length // chunk):
        at = slice(k * chunk, (k + 1) * chunk)
        field[:, at] = mm(steer, raw_ref[:, :, at].reshape(rows, chunk)).astype(BF16)

    def window(n, carry):
        at = pl.ds(pl.multiple_of(n * stride, stride), width)
        both = mm_last(taps[...], field[:, at])
        here = pl.ds(pl.multiple_of(n * quarter, quarter), quarter)
        polar_ref[here, :beams] = (both[:quarter, :beams] + both[quarter:, beams:]).astype(BF16)
        polar_ref[here, beams:] = (both[:quarter, beams:] - both[quarter:, :beams]).astype(BF16)
        return carry

    count = length // stride
    inner = count - 2
    lax.fori_loop(0, inner, window, 0, unroll=True)
    halo_copy.wait()
    tail = mm(steer, halo[...].reshape(rows, reach))
    tail = jnp.where(rng == 0, tail, jnp.zeros_like(tail))
    field[:, length:] = tail.astype(BF16)
    for n in range(inner, count):
        window(n, 0)
    for copy in copies:
        copy.wait()


def front(steering, chirp, raw, start, coef, rate):
    pulses, _, length = raw.shape
    reach = chirp.shape[1]
    sections = coef.shape[0]
    nodes = 2**sections
    beams = steering.shape[2]
    vmem = pl.BlockSpec(memory_space=pltpu.VMEM)
    dma = pltpu.SemaphoreType.DMA
    return pl.pallas_call(
        functools.partial(front_kernel, sections),
        in_specs=[vmem] * 6,
        out_specs=[vmem] * 3,
        out_shape=[
            jax.ShapeDtypeStruct((length // 2, 2 * beams), BF16),
            jax.ShapeDtypeStruct((nodes - 1, ROWS, beams), F32),
            jax.ShapeDtypeStruct((nodes // 2, sections, ROWS, beams), F32),
        ],
        scratch_shapes=[
            pltpu.VMEM((sections, ROWS, beams), F32),
            pltpu.VMEM((sections, ROWS, beams), F32),
            pltpu.VMEM((2 * beams, length + reach), BF16),
            pltpu.VMEM((pulses, 2, reach), BF16),
            pltpu.VMEM((2 * beams, 2 * pulses), BF16),
            pltpu.VMEM((reach // 2, 6 * (reach // 4)), BF16),
            dma((2,)),
            dma((nodes - 1,)),
            dma((nodes - 1,)),
            dma((nodes // 2,)),
            dma((nodes // 2,)),
        ],
        compiler_params=pltpu.CompilerParams(
            vmem_limit_bytes=60 * MIB, collective_id=0, has_side_effects=True
        ),
        cost_estimate=pl.CostEstimate(flops=4 * 10**9, bytes_accessed=7 * 10**6, transcendentals=0),
        name="front",
    )(steering, chirp, raw, start, coef, rate)


def turned(turns):
    whole = turns - lax.round(turns, lax.RoundingMethod.TO_NEAREST_EVEN)
    y = whole * math.pi
    y2 = y * y
    sine = jnp.full_like(y, -1.0 / math.factorial(11))
    for k in (9, 7, 5, 3, 1):
        sine = sine * y2 + (-1.0) ** (k // 2) / math.factorial(k)
    sine = sine * y
    cosine = jnp.full_like(y, 1.0 / math.factorial(12))
    for k in (10, 8, 6, 4, 2, 0):
        cosine = cosine * y2 + (-1.0) ** (k // 2) / math.factorial(k)
    return 1.0 - 2.0 * sine * sine, 2.0 * sine * cosine


def slots_kernel(tiles, place_ref, slot_ref):
    slots = place_ref.shape[1]

    def clear(n, carry):
        slot_ref[n] = slots
        return carry

    lax.fori_loop(0, slot_ref.shape[0], clear, 0, unroll=8)
    for c in range(place_ref.shape[0]):

        def enter(k, carry):
            at = 2 * (c * tiles + place_ref[c, k])
            at = at + (slot_ref[at] != slots).astype(jnp.int32)
            slot_ref[at] = k
            return carry

        lax.fori_loop(0, slots, enter, 0)


def slots_of(place, tiles):
    smem = pl.BlockSpec(memory_space=pltpu.SMEM)
    return pl.pallas_call(
        functools.partial(slots_kernel, tiles),
        in_specs=[smem],
        out_specs=smem,
        out_shape=jax.ShapeDtypeStruct((place.shape[0] * tiles * 2,), jnp.int32),
        cost_estimate=pl.CostEstimate(flops=1000, bytes_accessed=1000, transcendentals=0),
        name="slots",
    )(place)


def halving_orders(levels):
    first = list(range(levels))
    second = [0, 3, 1, 2] + first[4:] if levels > 3 else first
    return [first, second]


WINDOWS = ((15,), (11, 7), (13, 3), (9, 14), (10, 12), (5, 6), (8, 1), (2, 4))


def tree_kernel(
    sections,
    taps,
    slot_ref,
    polar_ref,
    map_hbm,
    turns_ref,
    owns_ref,
    maps_ref,
    kept_ref,
    came_ref,
    turn_ref,
    chain_ref,
    fine_ref,
    coarse_ref,
    fields,
    leaves,
    range_map,
    sent,
    got,
    parts,
    total,
    tiles_sent,
    tiles_got,
    map_sem,
    basis_send,
    basis_recv,
    tile_send,
    tile_recv,
):
    sub, rng = lax.axis_index("sub"), lax.axis_index("rng")
    nodes = 2**sections
    order = node_order(sections)
    bins, pair = polar_ref.shape
    beams = pair // 2
    tiles = tiles_got.shape[1]
    levels = top_bit(tiles)
    orders = halving_orders(levels)
    slots, _, tile_rows, _ = maps_ref.shape
    chunk = 512
    fetch = pltpu.make_async_copy(map_hbm, range_map, map_sem)
    fetch.start()
    barrier = pltpu.get_barrier_semaphore()
    reach = max(sections, levels - 1)
    friends = [(sub, 1 - rng)] + [(flipped(sub, 2**k), rng) for k in range(reach)]
    for friend in friends:
        pl.semaphore_signal(barrier, inc=1, device_id=friend, device_id_type=MESH)

    depth = lax.broadcasted_iota(jnp.int32, (beams, beams), 0).astype(F32)
    lane = lax.broadcasted_iota(jnp.int32, (LANES, beams), 0).astype(F32)
    blocks = bins // LANES
    first = lax.broadcasted_iota(jnp.int32, (blocks, beams), 0) * LANES + rng * bins
    first = first.astype(F32)

    def complex_of(data):
        offset = depth - data[2 * taps : 2 * taps + 1, :]
        real = jnp.zeros((beams, beams), F32)
        imag = jnp.zeros((beams, beams), F32)
        for t in range(taps):
            hit = offset == t
            real = jnp.where(hit, data[t : t + 1, :], real)
            imag = jnp.where(hit, data[taps + t : taps + t + 1, :], imag)
        upper = jnp.concatenate([real, imag], axis=1)
        lower = jnp.concatenate([-imag, real], axis=1)
        return jnp.concatenate([upper, lower], axis=0).astype(BF16)

    chains = {}

    def chain_of(e, s):
        if (e, s) not in chains:
            at = len(chains)
            own = complex_of(owns_ref[e, s])
            if s > top_bit(e) + 1:
                own = mm(chain_ref[chain_of(e, s - 1)], own).astype(BF16)
                at = len(chains)
            chains[(e, s)] = at
            chain_ref[at] = own
        return chains[(e, s)]

    def prepare(e):
        i, s = order.index(e), top_bit(e)
        parent = e ^ 2**s
        turn = complex_of(turns_ref[i])
        if s > top_bit(parent) + 1:
            turn = mm(chain_ref[chain_of(parent, s - 1)], turn).astype(BF16)
        turn_ref[i] = turn
        rate = turns_ref[i, 2 * taps + 1 : 2 * taps + 2, :]
        fine_ref[i, 0], fine_ref[i, 1] = turned(rate * lane * (1.0 / bins))
        coarse_ref[i, 0], coarse_ref[i, 1] = turned(rate * first * (1.0 / bins))

    def merge(i, source, target):
        def step(c, carry):
            base = pl.multiple_of(c * chunk, chunk)
            value = mm(source[pl.ds(base, chunk), :], turn_ref[i])
            fine_cos, fine_sin = fine_ref[i, 0], fine_ref[i, 1]
            for j in range(chunk // LANES):
                at = pl.ds(c * (chunk // LANES) + j, 1)
                cos, sin = coarse_ref[i, 0, at, :], coarse_ref[i, 1, at, :]
                cosine = fine_cos * cos - fine_sin * sin
                sine = fine_cos * sin + fine_sin * cos
                here = value[j * LANES : (j + 1) * LANES]
                real, imag = here[:, :beams], here[:, beams:]
                both = jnp.concatenate(
                    [real * cosine - imag * sine, real * sine + imag * cosine], axis=1
                )
                target[pl.ds(pl.multiple_of(base + j * LANES, LANES), LANES), :] = both.astype(BF16)
            return carry

        lax.fori_loop(0, bins // chunk, step, 0, unroll=True)

    def project(e, field):
        by_real = mm_first(field[...], range_map[0])
        by_imag = mm_first(field[...], range_map[1])
        basis = jnp.concatenate(
            [by_real[:beams] - by_imag[beams:], by_imag[:beams] + by_real[beams:]], axis=0
        )
        if e < nodes // 2:
            basis = mm_first(chain_ref[chain_of(e, sections - 1)], basis.astype(BF16))
        return basis

    def message(e):
        i = order.index(e)
        return pltpu.make_async_remote_copy(
            src_ref=sent.at[i],
            dst_ref=got.at[i],
            send_sem=basis_send.at[i],
            recv_sem=basis_recv.at[i],
            device_id=(flipped(sub, 2 ** low_bit(e)), rng),
            device_id_type=MESH,
        )

    def needed(e):
        return [e | 2**k for k in range(low_bit(e) if e else sections)]

    def gathered(e, basis):
        for other in needed(e):
            basis = basis + got[order.index(other)].astype(F32)
        return basis

    merged = {0: polar_ref}

    def field_of(e, leaf):
        if e not in merged:
            parent = field_of(e ^ 2 ** top_bit(e), leaf)
            prepare(e)
            target = fields.at[e - 1] if e < nodes // 2 else leaves.at[leaf]
            merge(order.index(e), parent, target)
            merged[e] = target
        return merged[e]

    window_of = {e: w for w, window in enumerate(WINDOWS) for e in window}
    for w, window in enumerate(WINDOWS):
        late = []
        for e in window:
            for other in needed(e):
                if window_of[other] < w - 1:
                    message(other).wait_recv()
                else:
                    late.append(other)
        if w == 0:
            field_of(window[0], 0)
            fetch.wait()
        bases = {}
        for n, e in enumerate(window):
            bases[e] = project(e, field_of(e, n))
            if not late:
                sent[order.index(e)] = gathered(e, bases[e]).astype(BF16)
        for other in late:
            message(other).wait_recv()
        if late:
            for e in window:
                sent[order.index(e)] = gathered(e, bases[e]).astype(BF16)
        if w == 0:
            pl.semaphore_wait(barrier, len(friends))
        for e in window:
            message(e).start()

    real = maps_ref[:, 0].reshape(slots * tile_rows, beams)
    imag = maps_ref[:, 1].reshape(slots * tile_rows, beams)
    basis = project(0, polar_ref)
    for other in needed(0):
        message(other).wait_recv()
    basis = gathered(0, basis).astype(BF16)
    shape = (slots, tile_rows, basis.shape[1])
    parts[0, :slots] = mm(jnp.concatenate([real, -imag], axis=1), basis).reshape(shape)
    parts[1, :slots] = mm(jnp.concatenate([imag, real], axis=1), basis).reshape(shape)
    parts[0, slots] = jnp.zeros(shape[1:], F32)
    parts[1, slots] = jnp.zeros(shape[1:], F32)

    def exchange(c, k):
        half = tiles >> (k + 1)
        bit = orders[c][k]
        there = (flipped(sub, 2 ** (bit - 1)), rng) if bit else (sub, 1 - rng)
        return pltpu.make_async_remote_copy(
            src_ref=tiles_sent.at[c, pl.ds(half, half)],
            dst_ref=tiles_got.at[c, pl.ds(half, half)],
            send_sem=tile_send.at[c, k],
            recv_sem=tile_recv.at[c, k],
            device_id=there,
            device_id_type=MESH,
        )

    def part_of(c, t):
        at = 2 * (c * tiles + t)
        return parts[c, slot_ref[at]] + parts[c, slot_ref[at + 1]]

    half = tiles // 2
    for c in range(2):

        def outer(t, carry):
            tiles_sent[c, t] = part_of(c, t).astype(BF16)
            return carry

        lax.fori_loop(half, tiles, outer, 0, unroll=4)
        exchange(c, 0).start()
    for c in range(2):

        def inner(t, carry):
            total[c, t] = part_of(c, t)
            return carry

        lax.fori_loop(0, half, inner, 0, unroll=4)
    for k in range(levels - 1):
        half = tiles >> (k + 1)
        quarter = half // 2
        for c in range(2):
            exchange(c, k).wait_recv()

            def upper(t, carry):
                value = total[c, t] + tiles_got[c, half + t].astype(F32)
                tiles_sent[c, t] = value.astype(BF16)
                return carry

            lax.fori_loop(quarter, half, upper, 0, unroll=min(4, quarter))
            exchange(c, k + 1).start()
        for c in range(2):

            def lower(t, carry):
                total[c, t] = total[c, t] + tiles_got[c, half + t].astype(F32)
                return carry

            lax.fori_loop(0, quarter, lower, 0, unroll=min(4, quarter))
    for c in range(2):
        exchange(c, levels - 1).wait_recv()
        kept_ref[c] = total[c, 0]
        came_ref[c] = tiles_got[c, 1]
    for e in order:
        message(e).wait_send()
    for c in range(2):
        for k in range(levels):
            exchange(c, k).wait_send()


def tree(slot_of, polar, range_map, turns, owns, maps, sections, taps, tiles):
    bins, pair = polar.shape
    beams = pair // 2
    nodes = 2**sections
    cols = range_map.shape[2]
    slots, _, tile_rows, _ = maps.shape
    levels = top_bit(tiles)
    vmem = pl.BlockSpec(memory_space=pltpu.VMEM)
    dma = pltpu.SemaphoreType.DMA
    tile = (tile_rows, cols)
    return pl.pallas_call(
        functools.partial(tree_kernel, sections, taps),
        in_specs=[pl.BlockSpec(memory_space=pltpu.SMEM), vmem, pl.BlockSpec(memory_space=pl.ANY)]
        + [vmem] * 3,
        out_specs=[vmem, vmem],
        out_shape=[
            jax.ShapeDtypeStruct((2,) + tile, F32),
            jax.ShapeDtypeStruct((2,) + tile, BF16),
        ],
        scratch_shapes=[
            pltpu.VMEM((nodes - 1, pair, pair), BF16),
            pltpu.VMEM((nodes - 1, pair, pair), BF16),
            pltpu.VMEM((nodes - 1, 2, LANES, beams), F32),
            pltpu.VMEM((nodes - 1, 2, bins // LANES, beams), F32),
            pltpu.VMEM((nodes // 2 - 1, bins, pair), BF16),
            pltpu.VMEM((2, bins, pair), BF16),
            pltpu.VMEM(range_map.shape, BF16),
            pltpu.VMEM((nodes - 1, pair, cols), BF16),
            pltpu.VMEM((nodes - 1, pair, cols), BF16),
            pltpu.VMEM((2, slots + 1) + tile, F32),
            pltpu.VMEM((2, tiles // 2) + tile, F32),
            pltpu.VMEM((2, tiles) + tile, BF16),
            pltpu.VMEM((2, tiles) + tile, BF16),
            dma,
            dma((nodes - 1,)),
            dma((nodes - 1,)),
            dma((2, levels)),
            dma((2, levels)),
        ],
        compiler_params=pltpu.CompilerParams(
            vmem_limit_bytes=60 * MIB, collective_id=1, has_side_effects=True
        ),
        cost_estimate=pl.CostEstimate(flops=26 * 10**9, bytes_accessed=12 * 10**6, transcendentals=0),
        name="tree",
    )(slot_of, polar, range_map, turns, owns, maps)


def shards(
    raw_echoes,
    chirp_replica,
    steering,
    band_start,
    band_coef,
    phase_rate,
    range_map,
    slot_maps,
    coverage,
):
    sections, _, _, _, band, _ = band_coef.shape
    cores = lax.axis_size("rng")
    tiles = lax.axis_size("sub") * cores
    me = lax.axis_index("sub") * cores + lax.axis_index("rng")
    levels = top_bit(tiles)
    away = coverage[:, 0] ^ me
    place = jnp.stack(
        [
            sum(((away >> bit) & 1) << (levels - 1 - k) for k, bit in enumerate(order))
            for order in halving_orders(levels)
        ]
    )
    slot_of = slots_of(place, tiles)
    polar, turns, owns = front(
        steering, chirp_replica, raw_echoes, band_start, band_coef, phase_rate
    )
    kept, came = tree(slot_of, polar, range_map, turns, owns, slot_maps, sections, band, tiles)
    return (kept + came.astype(F32))[None]


def solution(mesh):
    in_specs = (
        P("sub", None, "rng"),
        P(),
        P("sub", None, None, None),
        P(None, "sub", None, None),
        P(None, "sub", None, None, None, None),
        P(None, "sub", None),
        P(None, "rng", None),
        P(("sub", "rng"), None, None, None),
        P(("sub", "rng"), None),
    )
    out_specs = P(("sub", "rng"), None, None, None)
    return jax.shard_map(shards, mesh=mesh, in_specs=in_specs, out_specs=out_specs, check_vma=False)
```

```python
import functools
import math

import jax
import jax.numpy as jnp
from jax import lax
from jax.experimental import pallas as pl
from jax.experimental.pallas import tpu as pltpu
from jax.sharding import PartitionSpec as P

LANES = 128
ROWS = 24
F32 = jnp.float32
BF16 = jnp.bfloat16
MESH = pl.DeviceIdType.MESH
MIB = 1024 * 1024


def mm(a, b):
    return jnp.dot(a, b, preferred_element_type=F32)


def mm_first(a, b):
    return lax.dot_general(a, b, (((0,), (0,)), ((), ())), preferred_element_type=F32)


def mm_last(a, b):
    return lax.dot_general(a, b, (((1,), (1,)), ((), ())), preferred_element_type=F32)


def top_bit(e):
    return e.bit_length() - 1


def low_bit(e):
    return (e & -e).bit_length() - 1


def node_order(sections):
    return sorted(range(1, 2**sections), key=lambda e: (low_bit(e), e))


def flipped(index, mask):
    out = index
    for k in range(mask.bit_length()):
        if mask >> k & 1:
            out = out + 2**k * (1 - 2 * lax.rem(lax.div(index, 2**k), 2))
    return out


def meet(devices):
    barrier = pltpu.get_barrier_semaphore()
    for device in devices:
        pl.semaphore_signal(barrier, inc=1, device_id=device, device_id_type=MESH)
    pl.semaphore_wait(barrier, len(devices))


def front_kernel(
    sections,
    steer_ref,
    chirp_ref,
    raw_ref,
    start_ref,
    coef_ref,
    rate_ref,
    polar_ref,
    turns_all,
    owns_all,
    owns_here,
    turns_here,
    field,
    halo,
    steer_out,
    taps,
    halo_sems,
    turn_send,
    turn_recv,
    own_send,
    own_recv,
):
    sub, rng = lax.axis_index("sub"), lax.axis_index("rng")
    nodes = 2**sections
    order = node_order(sections)
    pulses, _, length = raw_ref.shape
    rows = 2 * pulses
    reach = halo.shape[2]
    beams = steer_ref.shape[2]
    band = coef_ref.shape[4]
    quarter = reach // 4
    stride = 2 * quarter
    width = 6 * quarter
    partner = (sub, 1 - rng)
    for s in range(sections):
        for j, packed in enumerate((owns_here, turns_here)):
            for c in range(2):
                packed[s, c * band : (c + 1) * band] = coef_ref[s, 0, j, c].astype(F32)
            packed[s, 2 * band :] = jnp.concatenate(
                [
                    start_ref[s, 0, j : j + 1].astype(F32),
                    rate_ref[s],
                    jnp.zeros((ROWS - 2 * band - 2, beams), F32),
                ],
                axis=0,
            )
    meet([partner] + [(flipped(sub, e), rng) for e in range(1, nodes)])
    copies = []
    halo_copy = pltpu.make_async_remote_copy(
        src_ref=raw_ref.at[:, :, pl.ds(0, reach)],
        dst_ref=halo,
        send_sem=halo_sems.at[0],
        recv_sem=halo_sems.at[1],
        device_id=partner,
        device_id_type=MESH,
    )
    halo_copy.start()
    for i, e in enumerate(order):
        top = top_bit(e)
        there = (flipped(sub, e), rng)
        copies.append(
            pltpu.make_async_remote_copy(
                src_ref=turns_here.at[top],
                dst_ref=turns_all.at[i],
                send_sem=turn_send.at[i],
                recv_sem=turn_recv.at[i],
                device_id=there,
                device_id_type=MESH,
            )
        )
        if top + 1 < sections:
            kept = pl.ds(top + 1, sections - top - 1)
            copies.append(
                pltpu.make_async_remote_copy(
                    src_ref=owns_here.at[kept],
                    dst_ref=owns_all.at[e, kept],
                    send_sem=own_send.at[e],
                    recv_sem=own_recv.at[e],
                    device_id=there,
                    device_id_type=MESH,
                )
            )
    for copy in copies:
        copy.start()
    owns_all[0] = owns_here[...]

    real, imag = steer_ref[0, 0], steer_ref[0, 1]
    apart = jnp.concatenate(
        [jnp.concatenate([real, -imag], axis=1), jnp.concatenate([imag, real], axis=1)], axis=0
    )
    source = lax.broadcasted_iota(jnp.int32, (rows, rows), 0)
    target = lax.broadcasted_iota(jnp.int32, (rows, rows), 1)
    place = jnp.where(source < pulses, 2 * source, 2 * (source - pulses) + 1)
    weave = (place == target).astype(F32).astype(BF16)
    steer_out[...] = mm(apart, weave).astype(BF16)
    for c in range(2):
        line = chirp_ref[c : c + 1, :].astype(F32)
        line = jnp.concatenate([line, jnp.zeros((1, width - reach), F32)], axis=1)
        tall = jnp.broadcast_to(line, (quarter, width))
        rolled = pltpu.roll(tall, 0, 1, stride=2, stride_axis=0)
        taps[c * quarter : (c + 1) * quarter, :] = rolled.astype(BF16)

    chunk = 4 * stride
    steer = steer_out[...]

    for k in range(length // chunk):
        at = slice(k * chunk, (k + 1) * chunk)
        field[:, at] = mm(steer, raw_ref[:, :, at].reshape(rows, chunk)).astype(BF16)

    def window(n, carry):
        at = pl.ds(pl.multiple_of(n * stride, stride), width)
        both = mm_last(taps[...], field[:, at])
        here = pl.ds(pl.multiple_of(n * quarter, quarter), quarter)
        polar_ref[here, :beams] = (both[:quarter, :beams] + both[quarter:, beams:]).astype(BF16)
        polar_ref[here, beams:] = (both[:quarter, beams:] - both[quarter:, :beams]).astype(BF16)
        return carry

    count = length // stride
    inner = count - 2
    lax.fori_loop(0, inner, window, 0, unroll=True)
    halo_copy.wait()
    tail = mm(steer, halo[...].reshape(rows, reach))
    tail = jnp.where(rng == 0, tail, jnp.zeros_like(tail))
    field[:, length:] = tail.astype(BF16)
    for n in range(inner, count):
        window(n, 0)
    for copy in copies:
        copy.wait()


def front(steering, chirp, raw, start, coef, rate):
    pulses, _, length = raw.shape
    reach = chirp.shape[1]
    sections = coef.shape[0]
    nodes = 2**sections
    beams = steering.shape[2]
    vmem = pl.BlockSpec(memory_space=pltpu.VMEM)
    dma = pltpu.SemaphoreType.DMA
    return pl.pallas_call(
        functools.partial(front_kernel, sections),
        in_specs=[vmem] * 6,
        out_specs=[vmem] * 3,
        out_shape=[
            jax.ShapeDtypeStruct((length // 2, 2 * beams), BF16),
            jax.ShapeDtypeStruct((nodes - 1, ROWS, beams), F32),
            jax.ShapeDtypeStruct((nodes // 2, sections, ROWS, beams), F32),
        ],
        scratch_shapes=[
            pltpu.VMEM((sections, ROWS, beams), F32),
            pltpu.VMEM((sections, ROWS, beams), F32),
            pltpu.VMEM((2 * beams, length + reach), BF16),
            pltpu.VMEM((pulses, 2, reach), BF16),
            pltpu.VMEM((2 * beams, 2 * pulses), BF16),
            pltpu.VMEM((reach // 2, 6 * (reach // 4)), BF16),
            dma((2,)),
            dma((nodes - 1,)),
            dma((nodes - 1,)),
            dma((nodes // 2,)),
            dma((nodes // 2,)),
        ],
        compiler_params=pltpu.CompilerParams(
            vmem_limit_bytes=60 * MIB, collective_id=0, has_side_effects=True
        ),
        cost_estimate=pl.CostEstimate(flops=4 * 10**9, bytes_accessed=7 * 10**6, transcendentals=0),
        name="front",
    )(steering, chirp, raw, start, coef, rate)


def turned(turns):
    whole = turns - lax.round(turns, lax.RoundingMethod.TO_NEAREST_EVEN)
    y = whole * math.pi
    y2 = y * y
    sine = jnp.full_like(y, -1.0 / math.factorial(11))
    for k in (9, 7, 5, 3, 1):
        sine = sine * y2 + (-1.0) ** (k // 2) / math.factorial(k)
    sine = sine * y
    cosine = jnp.full_like(y, 1.0 / math.factorial(12))
    for k in (10, 8, 6, 4, 2, 0):
        cosine = cosine * y2 + (-1.0) ** (k // 2) / math.factorial(k)
    return 1.0 - 2.0 * sine * sine, 2.0 * sine * cosine


def slots_kernel(tiles, place_ref, slot_ref):
    slots = place_ref.shape[1]

    def clear(n, carry):
        slot_ref[n] = slots
        return carry

    lax.fori_loop(0, slot_ref.shape[0], clear, 0, unroll=8)
    for c in range(place_ref.shape[0]):

        def enter(k, carry):
            at = 2 * (c * tiles + place_ref[c, k])
            at = at + (slot_ref[at] != slots).astype(jnp.int32)
            slot_ref[at] = k
            return carry

        lax.fori_loop(0, slots, enter, 0)


def slots_of(place, tiles):
    smem = pl.BlockSpec(memory_space=pltpu.SMEM)
    return pl.pallas_call(
        functools.partial(slots_kernel, tiles),
        in_specs=[smem],
        out_specs=smem,
        out_shape=jax.ShapeDtypeStruct((place.shape[0] * tiles * 2,), jnp.int32),
        cost_estimate=pl.CostEstimate(flops=1000, bytes_accessed=1000, transcendentals=0),
        name="slots",
    )(place)


def halving_orders(levels):
    first = list(range(levels))
    second = [0, 3, 1, 2] + first[4:] if levels > 3 else first
    return [first, second]


WINDOWS = ((15,), (11, 7), (13, 3), (9, 14), (10, 12), (5, 6), (8, 1), (2, 4))


def tree_kernel(
    sections,
    taps,
    slot_ref,
    polar_ref,
    map_hbm,
    turns_ref,
    owns_ref,
    maps_ref,
    kept_ref,
    came_ref,
    turn_ref,
    chain_ref,
    fine_ref,
    coarse_ref,
    fields,
    leaves,
    range_map,
    sent,
    got,
    parts,
    total,
    tiles_sent,
    tiles_got,
    map_sem,
    basis_send,
    basis_recv,
    tile_send,
    tile_recv,
):
    sub, rng = lax.axis_index("sub"), lax.axis_index("rng")
    nodes = 2**sections
    order = node_order(sections)
    bins, pair = polar_ref.shape
    beams = pair // 2
    tiles = tiles_got.shape[1]
    levels = top_bit(tiles)
    orders = halving_orders(levels)
    slots, _, tile_rows, _ = maps_ref.shape
    chunk = 512
    fetch = pltpu.make_async_copy(map_hbm, range_map, map_sem)
    fetch.start()
    barrier = pltpu.get_barrier_semaphore()
    reach = max(sections, levels - 1)
    friends = [(sub, 1 - rng)] + [(flipped(sub, 2**k), rng) for k in range(reach)]
    for friend in friends:
        pl.semaphore_signal(barrier, inc=1, device_id=friend, device_id_type=MESH)

    depth = lax.broadcasted_iota(jnp.int32, (beams, beams), 0).astype(F32)
    lane = lax.broadcasted_iota(jnp.int32, (LANES, beams), 0).astype(F32)
    blocks = bins // LANES
    first = lax.broadcasted_iota(jnp.int32, (blocks, beams), 0) * LANES + rng * bins
    first = first.astype(F32)

    def complex_of(data):
        offset = depth - data[2 * taps : 2 * taps + 1, :]
        real = jnp.zeros((beams, beams), F32)
        imag = jnp.zeros((beams, beams), F32)
        for t in range(taps):
            hit = offset == t
            real = jnp.where(hit, data[t : t + 1, :], real)
            imag = jnp.where(hit, data[taps + t : taps + t + 1, :], imag)
        upper = jnp.concatenate([real, imag], axis=1)
        lower = jnp.concatenate([-imag, real], axis=1)
        return jnp.concatenate([upper, lower], axis=0).astype(BF16)

    chains = {}

    def chain_of(e, s):
        if (e, s) not in chains:
            at = len(chains)
            own = complex_of(owns_ref[e, s])
            if s > top_bit(e) + 1:
                own = mm(chain_ref[chain_of(e, s - 1)], own).astype(BF16)
                at = len(chains)
            chains[(e, s)] = at
            chain_ref[at] = own
        return chains[(e, s)]

    def prepare(e):
        i, s = order.index(e), top_bit(e)
        parent = e ^ 2**s
        turn = complex_of(turns_ref[i])
        if s > top_bit(parent) + 1:
            turn = mm(chain_ref[chain_of(parent, s - 1)], turn).astype(BF16)
        turn_ref[i] = turn
        rate = turns_ref[i, 2 * taps + 1 : 2 * taps + 2, :]
        fine_ref[i, 0], fine_ref[i, 1] = turned(rate * lane * (1.0 / bins))
        coarse_ref[i, 0], coarse_ref[i, 1] = turned(rate * first * (1.0 / bins))

    def merge(i, source, target):
        def step(c, carry):
            base = pl.multiple_of(c * chunk, chunk)
            value = mm(source[pl.ds(base, chunk), :], turn_ref[i])
            fine_cos, fine_sin = fine_ref[i, 0], fine_ref[i, 1]
            for j in range(chunk // LANES):
                at = pl.ds(c * (chunk // LANES) + j, 1)
                cos, sin = coarse_ref[i, 0, at, :], coarse_ref[i, 1, at, :]
                cosine = fine_cos * cos - fine_sin * sin
                sine = fine_cos * sin + fine_sin * cos
                here = value[j * LANES : (j + 1) * LANES]
                real, imag = here[:, :beams], here[:, beams:]
                both = jnp.concatenate(
                    [real * cosine - imag * sine, real * sine + imag * cosine], axis=1
                )
                target[pl.ds(pl.multiple_of(base + j * LANES, LANES), LANES), :] = both.astype(BF16)
            return carry

        lax.fori_loop(0, bins // chunk, step, 0, unroll=True)

    def project(e, field):
        by_real = mm_first(range_map[0], field[...])
        by_imag = mm_first(range_map[1], field[...])
        basis = jnp.concatenate(
            [by_real[:, :beams] - by_imag[:, beams:], by_imag[:, :beams] + by_real[:, beams:]],
            axis=1,
        )
        return basis

    def chained(e, basis):
        if e < nodes // 2:
            basis = mm(basis.astype(BF16), chain_ref[chain_of(e, sections - 1)])
        return basis

    def message(e):
        i = order.index(e)
        return pltpu.make_async_remote_copy(
            src_ref=sent.at[i],
            dst_ref=got.at[i],
            send_sem=basis_send.at[i],
            recv_sem=basis_recv.at[i],
            device_id=(flipped(sub, 2 ** low_bit(e)), rng),
            device_id_type=MESH,
        )

    def needed(e):
        return [e | 2**k for k in range(low_bit(e) if e else sections)]

    def gathered(e, basis):
        for other in needed(e):
            basis = basis + got[order.index(other)].astype(F32)
        return basis

    merged = {0: polar_ref}
    prepared = {0}

    def ready(e):
        if e not in prepared:
            ready(e ^ 2 ** top_bit(e))
            prepare(e)
            prepared.add(e)

    def ahead(e):
        ready(e)
        if e < nodes // 2:
            chain_of(e, sections - 1)

    def field_of(e, leaf):
        if e not in merged:
            parent = field_of(e ^ 2 ** top_bit(e), leaf)
            ready(e)
            target = fields.at[e - 1] if e < nodes // 2 else leaves.at[leaf]
            merge(order.index(e), parent, target)
            merged[e] = target
        return merged[e]

    window_of = {e: w for w, window in enumerate(WINDOWS) for e in window}
    for w, window in enumerate(WINDOWS):
        late = []
        for e in window:
            for other in needed(e):
                if window_of[other] < w - 1:
                    message(other).wait_recv()
                else:
                    late.append(other)
        if w == 0:
            field_of(window[0], 0)
            fetch.wait()
        bases = {}
        def finish(e):
            bases[e] = chained(e, bases[e])
            if not late:
                sent[order.index(e)] = gathered(e, bases[e]).astype(BF16)

        for n, e in enumerate(window):
            field = field_of(e, n)
            if n:
                finish(window[n - 1])
            if n == len(window) - 1:
                for other in (WINDOWS + ((0,),))[w + 1]:
                    ahead(other)
            bases[e] = project(e, field)
        finish(window[-1])
        for other in late:
            message(other).wait_recv()
        if late:
            for e in window:
                sent[order.index(e)] = gathered(e, bases[e]).astype(BF16)
        if w == 0:
            pl.semaphore_wait(barrier, len(friends))
        for e in window:
            message(e).start()

    real = maps_ref[:, 0].reshape(slots * tile_rows, beams)
    imag = maps_ref[:, 1].reshape(slots * tile_rows, beams)
    basis = chained(0, project(0, polar_ref))
    for other in needed(0):
        message(other).wait_recv()
    basis = gathered(0, basis).astype(BF16)
    shape = (slots, tile_rows, basis.shape[0])
    parts[0, :slots] = mm_last(jnp.concatenate([real, -imag], axis=1), basis).reshape(shape)
    parts[1, :slots] = mm_last(jnp.concatenate([imag, real], axis=1), basis).reshape(shape)
    parts[0, slots] = jnp.zeros(shape[1:], F32)
    parts[1, slots] = jnp.zeros(shape[1:], F32)

    def exchange(c, k):
        half = tiles >> (k + 1)
        bit = orders[c][k]
        there = (flipped(sub, 2 ** (bit - 1)), rng) if bit else (sub, 1 - rng)
        return pltpu.make_async_remote_copy(
            src_ref=tiles_sent.at[c, pl.ds(half, half)],
            dst_ref=tiles_got.at[c, pl.ds(half, half)],
            send_sem=tile_send.at[c, k],
            recv_sem=tile_recv.at[c, k],
            device_id=there,
            device_id_type=MESH,
        )

    def part_of(c, t):
        at = 2 * (c * tiles + t)
        return parts[c, slot_ref[at]] + parts[c, slot_ref[at + 1]]

    half = tiles // 2
    for c in range(2):

        def outer(t, carry):
            tiles_sent[c, t] = part_of(c, t).astype(BF16)
            return carry

        lax.fori_loop(half, tiles, outer, 0, unroll=4)
        exchange(c, 0).start()
    for c in range(2):

        def inner(t, carry):
            total[c, t] = part_of(c, t)
            return carry

        lax.fori_loop(0, half, inner, 0, unroll=4)
    for k in range(levels - 1):
        half = tiles >> (k + 1)
        quarter = half // 2
        for c in range(2):
            exchange(c, k).wait_recv()

            def upper(t, carry):
                value = total[c, t] + tiles_got[c, half + t].astype(F32)
                tiles_sent[c, t] = value.astype(BF16)
                return carry

            lax.fori_loop(quarter, half, upper, 0, unroll=min(4, quarter))
            exchange(c, k + 1).start()
        for c in range(2):

            def lower(t, carry):
                total[c, t] = total[c, t] + tiles_got[c, half + t].astype(F32)
                return carry

            lax.fori_loop(0, quarter, lower, 0, unroll=min(4, quarter))
    for c in range(2):
        exchange(c, levels - 1).wait_recv()
        kept_ref[c] = total[c, 0]
        came_ref[c] = tiles_got[c, 1]
    for e in order:
        message(e).wait_send()
    for c in range(2):
        for k in range(levels):
            exchange(c, k).wait_send()


def tree(slot_of, polar, range_map, turns, owns, maps, sections, taps, tiles):
    bins, pair = polar.shape
    beams = pair // 2
    nodes = 2**sections
    cols = range_map.shape[2]
    slots, _, tile_rows, _ = maps.shape
    levels = top_bit(tiles)
    vmem = pl.BlockSpec(memory_space=pltpu.VMEM)
    dma = pltpu.SemaphoreType.DMA
    tile = (tile_rows, cols)
    return pl.pallas_call(
        functools.partial(tree_kernel, sections, taps),
        in_specs=[pl.BlockSpec(memory_space=pltpu.SMEM), vmem, pl.BlockSpec(memory_space=pl.ANY)]
        + [vmem] * 3,
        out_specs=[vmem, vmem],
        out_shape=[
            jax.ShapeDtypeStruct((2,) + tile, F32),
            jax.ShapeDtypeStruct((2,) + tile, BF16),
        ],
        scratch_shapes=[
            pltpu.VMEM((nodes - 1, pair, pair), BF16),
            pltpu.VMEM((nodes - 1, pair, pair), BF16),
            pltpu.VMEM((nodes - 1, 2, LANES, beams), F32),
            pltpu.VMEM((nodes - 1, 2, bins // LANES, beams), F32),
            pltpu.VMEM((nodes // 2 - 1, bins, pair), BF16),
            pltpu.VMEM((2, bins, pair), BF16),
            pltpu.VMEM(range_map.shape, BF16),
            pltpu.VMEM((nodes - 1, cols, pair), BF16),
            pltpu.VMEM((nodes - 1, cols, pair), BF16),
            pltpu.VMEM((2, slots + 1) + tile, F32),
            pltpu.VMEM((2, tiles // 2) + tile, F32),
            pltpu.VMEM((2, tiles) + tile, BF16),
            pltpu.VMEM((2, tiles) + tile, BF16),
            dma,
            dma((nodes - 1,)),
            dma((nodes - 1,)),
            dma((2, levels)),
            dma((2, levels)),
        ],
        compiler_params=pltpu.CompilerParams(
            vmem_limit_bytes=60 * MIB, collective_id=1, has_side_effects=True
        ),
        cost_estimate=pl.CostEstimate(flops=26 * 10**9, bytes_accessed=12 * 10**6, transcendentals=0),
        name="tree",
    )(slot_of, polar, range_map, turns, owns, maps)


def shards(
    raw_echoes,
    chirp_replica,
    steering,
    band_start,
    band_coef,
    phase_rate,
    range_map,
    slot_maps,
    coverage,
):
    sections, _, _, _, band, _ = band_coef.shape
    cores = lax.axis_size("rng")
    tiles = lax.axis_size("sub") * cores
    me = lax.axis_index("sub") * cores + lax.axis_index("rng")
    levels = top_bit(tiles)
    away = coverage[:, 0] ^ me
    place = jnp.stack(
        [
            sum(((away >> bit) & 1) << (levels - 1 - k) for k, bit in enumerate(order))
            for order in halving_orders(levels)
        ]
    )
    slot_of = slots_of(place, tiles)
    polar, turns, owns = front(
        steering, chirp_replica, raw_echoes, band_start, band_coef, phase_rate
    )
    kept, came = tree(slot_of, polar, range_map, turns, owns, slot_maps, sections, band, tiles)
    return (kept + came.astype(F32))[None]


def solution(mesh):
    in_specs = (
        P("sub", None, "rng"),
        P(),
        P("sub", None, None, None),
        P(None, "sub", None, None),
        P(None, "sub", None, None, None, None),
        P(None, "sub", None),
        P(None, "rng", None),
        P(("sub", "rng"), None, None, None),
        P(("sub", "rng"), None),
    )
    out_specs = P(("sub", "rng"), None, None, None)
    return jax.shard_map(shards, mesh=mesh, in_specs=in_specs, out_specs=out_specs, check_vma=False)
```
